128 devices in a mesh: dp: 8 (over y, z_hi), seq: 16 (over z_lo, x, core).
Axes of the slice: x: 4, y: 4, z: 4 (z_hi: 2, z_lo: 2; z = z_hi * 2 + z_lo), core: 2. Of those that a mesh axis runs over, the one named last changes fastest.
Arguments:
- frames: bfloat16 [8, 256, 256, 1280], P('dp', 'seq'), may hold values from -6 to 6
- map_weight: bfloat16 [1280, 8], replicated, may hold values from -0.15625 to 0.15625
- qkv_weight: bfloat16 [1280, 3840], replicated, may hold values from -8 to 8, as said below
- cotangent: bfloat16 [8, 2048, 1280], P('dp', 'seq'), may hold values from -6 to 6
Outputs:
- grad_qkv_weight: float32 [1280, 3840], P(None, 'seq')
The draws below stay inside these ranges and needn't reach their ends.
Inputs may be any that keep to these rules, and one draw needn't show every extreme that they name: qkv_weight has mean zero and entries of order 1280 ** -0.5 times at most 40.
All inputs are finite; a program needn't handle non-finite values.
Results may differ from the reference program's by a relative error of at most 0.019.
Values may be sent and summed in bfloat16 or wider, within the bound.
No kernel may reach another device: no remote copies, remote signals or barrier semaphores. Data moves between devices by JAX's collectives and lax.ppermute only.
A program may use at most 128 MiB of HBM per device.

```python
import math
import jax
import jax.numpy as jnp
from jax import lax

HEADS = 16
HEAD_DIM = 80
D = 1280
PATCHES = 256
SLOTS = 8
CLIPS = 8
CLIP_FRAMES = 256
CLIP_TOKENS = 2048


def draw_qkv_weight(key, part):
    values = jax.random.normal(jax.random.fold_in(key, 11), (D, HEADS, 3, HEAD_DIM), jnp.float32) / math.sqrt(D)
    return jnp.clip(values, -8.0, 8.0).reshape(D, 3 * D).astype(jnp.bfloat16)


def with_spikes(array, stream_key, source, target, shards_of, factor):
    def block_of(axis_at):
        return (jnp.arange(array.shape[axis_at]) // (array.shape[axis_at] // shards_of)).reshape((-1,) + (1,) * (array.ndim - 1 - axis_at))

    first = jax.random.permutation(stream_key, shards_of)[block_of(target)]
    far = (block_of(target) + shards_of // 2) % shards_of
    return jnp.where((block_of(source) == first) | (block_of(source) == far), factor * array, array)


def block_scale(own_key, extent, pieces, smallest, top_value):
    factor_of, own = 1.0, jax.random.fold_in(own_key, 6)
    for axis_at, parts in pieces:
        steps = jnp.exp(jax.random.uniform(jax.random.fold_in(own, axis_at), (parts,), jnp.float32, smallest / len(pieces), top_value / len(pieces)))
        factor_of = factor_of * jnp.repeat(steps, extent[axis_at] // parts).reshape([-1 if axis == axis_at else 1 for axis in range(len(extent))])
    return factor_of


def gaussian(own_key, shape, width, reach, pieces=(), dtype=jnp.bfloat16):
    drawn = width * jax.random.normal(own_key, shape, jnp.float32)
    if pieces:
        drawn = drawn * block_scale(own_key, shape, pieces, -0.22, 0.18)
    return jnp.clip(drawn, -reach, reach).astype(dtype)


def gaussian_with(own_key, dims, scale, most, shards, heavy, kind=jnp.bfloat16):
    values = scale * jax.random.normal(own_key, dims, jnp.float32)
    if shards:
        values = values * block_scale(own_key, dims, shards, -0.22, 0.18)
    return jnp.clip(with_spikes(values, jax.random.fold_in(own_key, 3), *heavy), -most, most).astype(kind)


def setup_inputs(seed: int = 0) -> dict:
    key_list = jax.random.split(jax.random.key(seed), 5)
    frames = gaussian(key_list[0], (CLIPS, CLIP_FRAMES, PATCHES, D), 1.0, 6.0, ((0, 8), (1, 16)))
    map_weight = gaussian(key_list[1], (D, SLOTS), D ** -0.5, 0.15625)
    qkv_weight = draw_qkv_weight(jax.random.fold_in(key_list[4], 71), 0)
    cotangent = gaussian_with(key_list[3], (CLIPS, CLIP_TOKENS, D), 1.0, 6.0, ((0, 8), (1, 16)), (1, 2, 16, 2.0))
    return dict(frames=frames, map_weight=map_weight, qkv_weight=qkv_weight, cotangent=cotangent)


def learn_tokens(clip_frames, map_weight, qkv_weight):
    flat = clip_frames.reshape(-1, D)
    logits = jnp.dot(flat, map_weight, preferred_element_type=jnp.float32)
    token_maps = jax.nn.sigmoid(logits).astype(jnp.bfloat16).reshape(CLIP_FRAMES, PATCHES, SLOTS)
    pooled = jnp.einsum('fps,fpd->fsd', token_maps.astype(jnp.float32), clip_frames.astype(jnp.float32))
    pooled = pooled.reshape(CLIP_TOKENS, D)
    centred = pooled - lax.optimization_barrier(jnp.mean(pooled, axis=-1, keepdims=True))
    variance = lax.optimization_barrier(jnp.mean(centred * centred, axis=-1, keepdims=True))
    normed = (centred * lax.rsqrt(variance + 1e-06)).astype(jnp.bfloat16)
    projected = jnp.dot(normed, qkv_weight, preferred_element_type=jnp.float32).astype(jnp.bfloat16)
    return (normed, projected)

def head_grad(operands):
    rows, upstream = operands
    scaling = 1.0 / math.sqrt(HEAD_DIM)
    query_rows = rows[:, 0]
    key_rows = rows[:, 1]
    value_rows = rows[:, 2]
    scores = jnp.dot(query_rows, key_rows.T, preferred_element_type=jnp.float32) * scaling
    shifted = jnp.exp(scores - lax.optimization_barrier(jnp.max(scores, axis=-1, keepdims=True)))
    attention = shifted / lax.optimization_barrier(jnp.sum(shifted, axis=-1, keepdims=True))
    rounded = attention.astype(jnp.bfloat16)
    attended = jnp.dot(rounded, value_rows, preferred_element_type=jnp.float32)
    row_dot = lax.optimization_barrier(jnp.sum(upstream.astype(jnp.float32) * attended, axis=-1, keepdims=True))
    grad_attention = jnp.dot(upstream, value_rows.T, preferred_element_type=jnp.float32)
    grad_scores = (attention * (grad_attention - row_dot) * scaling).astype(jnp.bfloat16)
    grad_query = jnp.dot(grad_scores, key_rows, preferred_element_type=jnp.float32).astype(jnp.bfloat16)
    grad_key = jnp.dot(grad_scores.T, query_rows, preferred_element_type=jnp.float32).astype(jnp.bfloat16)
    grad_value = jnp.dot(rounded.T, upstream, preferred_element_type=jnp.float32).astype(jnp.bfloat16)
    return jnp.stack([grad_query, grad_key, grad_value], axis=1)

def reference(frames, map_weight, qkv_weight, cotangent):
    normed, projected = lax.map(lambda clip_frames: learn_tokens(clip_frames, map_weight, qkv_weight), frames)
    stacked = projected.reshape(CLIPS, CLIP_TOKENS, HEADS, 3, HEAD_DIM).transpose(0, 2, 1, 3, 4)
    stacked = stacked.reshape(CLIPS * HEADS, CLIP_TOKENS, 3, HEAD_DIM)
    upstream = cotangent.reshape(CLIPS, CLIP_TOKENS, HEADS, HEAD_DIM).transpose(0, 2, 1, 3)
    upstream = upstream.reshape(CLIPS * HEADS, CLIP_TOKENS, HEAD_DIM)
    grads = lax.map(head_grad, (stacked, upstream))
    grads = grads.reshape(CLIPS, HEADS, CLIP_TOKENS, 3, HEAD_DIM).transpose(0, 2, 1, 3, 4)
    grads = grads.reshape(CLIPS * CLIP_TOKENS, 3 * D)
    return jnp.dot(normed.reshape(-1, D).T, grads, preferred_element_type=jnp.float32)
```

```python
import functools
import math

import jax
import jax.numpy as jnp
from jax import lax
from jax.experimental import pallas as pl
from jax.experimental.pallas import tpu as pltpu
from jax.sharding import PartitionSpec as P

HEAD_DIM = 80
F32, BF16 = jnp.float32, jnp.bfloat16
LANES = 128


def matmul(a, b, dims=((1,), (0,))):
    return lax.dot_general(a, b, (dims, ((), ())), preferred_element_type=F32)


def thirds(value):
    high = value.astype(BF16)
    rest = value - high.astype(F32)
    middle = rest.astype(BF16)
    return high, middle, (rest - middle.astype(F32)).astype(BF16)


def learn_tokens(frames, map_weight):
    frame_count = frames.shape[0]
    width_all = frames.shape[2]
    logits = jnp.dot(frames.reshape(-1, width_all), map_weight, preferred_element_type=F32)
    token_maps = jax.nn.sigmoid(logits).astype(BF16).reshape(frame_count, frames.shape[1], -1)
    pooled = jnp.einsum("fps,fpd->fsd", token_maps, frames, preferred_element_type=F32)
    pooled = pooled.reshape(-1, width_all)
    centred = pooled - jnp.mean(pooled, axis=-1, keepdims=True)
    variance = jnp.mean(centred * centred, axis=-1, keepdims=True)
    return (centred * lax.rsqrt(variance + 1e-06)).astype(BF16)


def attention_kernel(step_rows, sub_rows, qkv_ref, cot_ref, out_ref, x, c, k3, v1, dk, dv):
    step = pl.program_id(0)
    hd = HEAD_DIM
    scale = 1.0 / math.sqrt(hd)
    pieces, _, width = qkv_ref.shape

    @pl.when(step == 0)
    def _():
        for piece in range(pieces):
            columns = slice(piece * width, (piece + 1) * width)
            x[:, columns] = qkv_ref[piece]
            c[:, columns] = cot_ref[piece]
        key = x[hd : 2 * hd, :]
        k3[...] = jnp.concatenate([key, key, key], axis=0)
        row = lax.broadcasted_iota(jnp.int32, (LANES - hd, pieces * width), 0)
        ones = jnp.where(row < 3, 1.0, 0.0).astype(BF16)
        v1[...] = jnp.concatenate([x[2 * hd : 3 * hd, :], ones], axis=0)
        dk[...] = jnp.zeros_like(dk)
        dv[...] = jnp.zeros_like(dv)

    lane = lax.broadcasted_iota(jnp.int32, (sub_rows, LANES - hd), 1)
    for sub in range(step_rows // sub_rows):
        rows = pl.ds(pl.multiple_of(step * step_rows + sub * sub_rows, sub_rows), sub_rows)
        query_t = x[0:hd, rows].astype(F32)
        cot_t = c[:, rows]
        cot = cot_t.T
        terms = jnp.concatenate(thirds(query_t * (scale * math.log2(math.e))), axis=0).T
        scores = matmul(terms, k3[...])
        shifted = jnp.exp2(scores - jnp.max(scores, axis=-1, keepdims=True)).astype(BF16)
        attended = matmul(shifted, v1[...], ((1,), (1,)))
        inverse = 1.0 / attended[:, hd : hd + 1]
        row_dot = jnp.sum(cot.astype(F32) * attended[:, 0:hd], axis=-1, keepdims=True) * inverse
        first, second, third = (t.astype(F32) for t in thirds(-row_dot))
        tail = jnp.where(
            lane == 0, first, jnp.where(lane == 1, second, jnp.where(lane == 2, third, 0.0))
        ).astype(BF16)
        difference = matmul(jnp.concatenate([cot, tail], axis=1), v1[...])
        grad_scores = (shifted.astype(F32) * difference).astype(BF16)
        grad_query = matmul(grad_scores, k3[0:hd, :], ((1,), (1,))) * (inverse * scale)
        out_ref[0:hd, rows] = grad_query.T.astype(BF16)
        inverse_t = jnp.broadcast_to(inverse, (sub_rows, LANES)).T[0:1, :]
        dk[...] += matmul((query_t * (inverse_t * scale)).astype(BF16), grad_scores)
        dv[...] += matmul((cot_t.astype(F32) * inverse_t).astype(BF16), shifted)

    @pl.when(step == pl.num_programs(0) - 1)
    def _():
        out_ref[hd : 2 * hd, :] = dk[...].astype(BF16)
        out_ref[2 * hd : 3 * hd, :] = dv[...].astype(BF16)


def attention_gradient(qkv, cot):
    pieces, columns, width = qkv.shape
    tokens = pieces * width
    step_rows, sub_rows = min(1024, tokens), min(256, tokens)
    whole = lambda shape: pl.BlockSpec(shape, lambda i: (0,) * len(shape))
    return pl.pallas_call(
        functools.partial(attention_kernel, step_rows, sub_rows),
        out_shape=jax.ShapeDtypeStruct((columns, tokens), BF16),
        grid=(tokens // step_rows,),
        in_specs=[whole(qkv.shape), whole(cot.shape)],
        out_specs=whole((columns, tokens)),
        scratch_shapes=[
            pltpu.VMEM((columns, tokens), BF16),
            pltpu.VMEM((HEAD_DIM, tokens), BF16),
            pltpu.VMEM((3 * HEAD_DIM, tokens), BF16),
            pltpu.VMEM((LANES, tokens), BF16),
            pltpu.VMEM((HEAD_DIM, tokens), F32),
            pltpu.VMEM((HEAD_DIM, tokens), F32),
        ],
        compiler_params=pltpu.CompilerParams(vmem_limit_bytes=48 << 20),
        cost_estimate=pl.CostEstimate(
            flops=12 * tokens * tokens * 128, bytes_accessed=4 << 20, transcendentals=tokens * tokens
        ),
        name="attention_gradient",
    )(qkv, cot)


def exchange(array, axis_name):
    return lax.all_to_all(array, axis_name, split_axis=0, concat_axis=0, tiled=True)


def body(frames, map_weight, qkv_weight, cotangent):
    seq, dp = lax.axis_size("seq"), lax.axis_size("dp")
    cot = exchange(cotangent[0].T.reshape(seq, -1, cotangent.shape[1]), "seq")
    normed = learn_tokens(frames[0], map_weight)
    projected = jnp.dot(normed, qkv_weight, preferred_element_type=F32).astype(BF16)
    qkv = exchange(projected.T.reshape(seq, -1, normed.shape[0]), "seq")
    tokens = lax.all_gather(normed, "seq", tiled=True)
    grads = attention_gradient(qkv, cot)
    term = matmul(grads, tokens).T.astype(BF16)
    pieces = exchange(term.reshape(dp, -1, term.shape[1]), "dp")
    summed = jnp.sum(pieces.astype(F32), axis=0).astype(BF16)
    whole = exchange(jnp.broadcast_to(summed[None], (dp,) + summed.shape), "dp")
    return whole.reshape(term.shape).astype(F32)


def solution(mesh):
    placed = (P("dp", "seq", None, None), P(), P(), P("dp", "seq", None))
    return jax.shard_map(
        body, mesh=mesh, in_specs=placed, out_specs=P(None, "seq"), check_vma=False
    )
```

```python
import functools
import math

import jax
import jax.numpy as jnp
from jax import lax
from jax.experimental import pallas as pl
from jax.experimental.pallas import tpu as pltpu
from jax.sharding import PartitionSpec as P

HEAD_DIM = 80
F32, BF16 = jnp.float32, jnp.bfloat16
LANES = 128


def matmul(a, b, dims=((1,), (0,))):
    return lax.dot_general(a, b, (dims, ((), ())), preferred_element_type=F32)


def thirds(value):
    high = value.astype(BF16)
    rest = value - high.astype(F32)
    middle = rest.astype(BF16)
    return high, middle, (rest - middle.astype(F32)).astype(BF16)


def tokens_kernel(
    group, frames, map_weight, weight, cot, normed, send, held, weight_held, map_weight_t, cot_held, sems, weight_sem
):
    count, _, width = frames.shape
    heads, rows, _ = send.shape
    own = weight.shape[1] // heads
    slots = map_weight_t.shape[0]
    parts = [pl.ds(g * group, group) for g in range(count // group)]
    loads = [
        pltpu.make_async_copy(frames.at[part], held.at[part], sems.at[g])
        for g, part in enumerate(parts)
    ]
    weight_load = pltpu.make_async_copy(weight, weight_held, weight_sem.at[0])
    map_load = pltpu.make_async_copy(map_weight, map_weight_t, weight_sem.at[1])
    cot_load = pltpu.make_async_copy(cot, cot_held, weight_sem.at[2])
    for load in (map_load, *loads, cot_load):
        load.start()
    map_load.wait()
    for g, load in enumerate(loads):
        load.wait()
        if g == 0:
            weight_load.start()
        blocks = [held[g * group + k] for k in range(group)]
        logits = [matmul(map_weight_t[...], block, ((1,), (1,))) for block in blocks]
        maps = [jax.nn.sigmoid(l).astype(BF16) for l in logits]
        pooled = jnp.concatenate([matmul(m, block) for m, block in zip(maps, blocks)], axis=0)
        centred = pooled - jnp.mean(pooled, axis=-1, keepdims=True)
        variance = jnp.mean(centred * centred, axis=-1, keepdims=True)
        at = g * group * slots
        normed[at : at + group * slots, :] = (centred * lax.rsqrt(variance + 1e-06)).astype(BF16)
    cot_load.wait()
    cot_t = cot_held[...].T
    for h in range(heads):
        send[h, own:rows, :] = cot_t[h * (rows - own) : (h + 1) * (rows - own), :]
    tokens = normed[...]
    weight_load.wait()
    for start in range(0, weight.shape[1], 256):
        block = matmul(tokens, weight_held[:, start : start + 256]).T.astype(BF16)
        at = start
        while at < start + 256:
            h = at // own
            end = min((h + 1) * own, start + 256)
            send[h, at - h * own : end - h * own, :] = block[at - start : end - start, :]
            at = end


def learn_tokens(frames, map_weight, weight, cot, heads):
    count, patches, width = frames.shape
    tokens, columns = cot.shape[0], weight.shape[1]
    group = math.gcd(count, 4)
    vmem, hbm = pl.BlockSpec(memory_space=pltpu.VMEM), pl.BlockSpec(memory_space=pltpu.HBM)
    return pl.pallas_call(
        functools.partial(tokens_kernel, group),
        out_shape=(
            jax.ShapeDtypeStruct((tokens, width), BF16),
            jax.ShapeDtypeStruct((heads, (columns + width) // heads, tokens), BF16),
        ),
        in_specs=[hbm, hbm, hbm, hbm],
        out_specs=(vmem, vmem),
        scratch_shapes=[
            pltpu.VMEM(frames.shape, BF16),
            pltpu.VMEM(weight.shape, BF16),
            pltpu.VMEM(map_weight.shape[::-1], BF16),
            pltpu.VMEM(cot.shape, BF16),
            pltpu.SemaphoreType.DMA((count // group,)),
            pltpu.SemaphoreType.DMA((3,)),
        ],
        compiler_params=pltpu.CompilerParams(vmem_limit_bytes=48 << 20),
        name="learn_tokens",
    )(frames, map_weight.T, weight, cot)


def weight_kernel(grads_ref, tokens, out_ref, held, sems):
    chunks = sems.shape[0]
    block = tokens.shape[0] // chunks
    parts = [pl.ds(i * block, block) for i in range(chunks)]
    loads = [pltpu.make_async_copy(tokens.at[p], held.at[p], sems.at[i]) for i, p in enumerate(parts)]
    for load in loads:
        load.start()
    total = None
    for part, load in zip(parts, loads):
        load.wait()
        term = matmul(grads_ref[:, part], held[part, :])
        total = term if total is None else total + term
    out_ref[...] = total.astype(BF16)


def weight_gradient(grads, tokens):
    vmem, hbm = pl.BlockSpec(memory_space=pltpu.VMEM), pl.BlockSpec(memory_space=pltpu.HBM)
    return pl.pallas_call(
        weight_kernel,
        out_shape=jax.ShapeDtypeStruct((grads.shape[0], tokens.shape[1]), BF16),
        in_specs=[vmem, hbm],
        out_specs=vmem,
        scratch_shapes=[pltpu.VMEM(tokens.shape, BF16), pltpu.SemaphoreType.DMA((4,))],
        compiler_params=pltpu.CompilerParams(vmem_limit_bytes=32 << 20),
        name="weight_gradient",
    )(grads, tokens)


def attention_kernel(step_rows, sub_rows, x_ref, out_ref, x, k3, v1, dk, dv):
    step = pl.program_id(0)
    hd = HEAD_DIM
    scale = 1.0 / math.sqrt(hd)
    pieces, _, width = x_ref.shape

    @pl.when(step == 0)
    def _():
        for piece in range(pieces):
            columns = slice(piece * width, (piece + 1) * width)
            x[:, columns] = x_ref[piece]
        key = x[hd : 2 * hd, :]
        k3[...] = jnp.concatenate([key, key, key], axis=0)
        row = lax.broadcasted_iota(jnp.int32, (LANES - hd, pieces * width), 0)
        ones = jnp.where(row < 3, 1.0, 0.0).astype(BF16)
        v1[...] = jnp.concatenate([x[2 * hd : 3 * hd, :], ones], axis=0)
        dk[...] = jnp.zeros_like(dk)
        dv[...] = jnp.zeros_like(dv)

    lane = lax.broadcasted_iota(jnp.int32, (sub_rows, LANES - hd), 1)
    for sub in range(step_rows // sub_rows):
        rows = pl.ds(pl.multiple_of(step * step_rows + sub * sub_rows, sub_rows), sub_rows)
        query_t = x[0:hd, rows].astype(F32)
        cot_t = x[3 * hd :, rows]
        cot = cot_t.T
        terms = jnp.concatenate(thirds(query_t * (scale * math.log2(math.e))), axis=0).T
        scores = matmul(terms, k3[...])
        shifted = jnp.exp2(scores - jnp.max(scores, axis=-1, keepdims=True)).astype(BF16)
        attended = matmul(shifted, v1[...], ((1,), (1,)))
        inverse = 1.0 / attended[:, hd : hd + 1]
        row_dot = jnp.sum(cot.astype(F32) * attended[:, 0:hd], axis=-1, keepdims=True) * inverse
        first, second, third = (t.astype(F32) for t in thirds(-row_dot))
        tail = jnp.where(
            lane == 0, first, jnp.where(lane == 1, second, jnp.where(lane == 2, third, 0.0))
        ).astype(BF16)
        difference = matmul(jnp.concatenate([cot, tail], axis=1), v1[...])
        grad_scores = (shifted.astype(F32) * difference).astype(BF16)
        grad_query = matmul(grad_scores, k3[0:hd, :], ((1,), (1,))) * (inverse * scale)
        out_ref[0:hd, rows] = grad_query.T.astype(BF16)
        inverse_t = jnp.broadcast_to(inverse, (sub_rows, LANES)).T[0:1, :]
        dk[...] += matmul((query_t * (inverse_t * scale)).astype(BF16), grad_scores)
        dv[...] += matmul((cot_t.astype(F32) * inverse_t).astype(BF16), shifted)

    @pl.when(step == pl.num_programs(0) - 1)
    def _():
        out_ref[hd : 2 * hd, :] = dk[...].astype(BF16)
        out_ref[2 * hd : 3 * hd, :] = dv[...].astype(BF16)
        out_ref[3 * hd :, :] = jnp.zeros((out_ref.shape[0] - 3 * hd, out_ref.shape[1]), BF16)


def attention_gradient(x, rows):
    pieces, columns, width = x.shape
    tokens = pieces * width
    step_rows, sub_rows = min(1024, tokens), min(256, tokens)
    whole = lambda shape: pl.BlockSpec(shape, lambda i: (0,) * len(shape))
    return pl.pallas_call(
        functools.partial(attention_kernel, step_rows, sub_rows),
        out_shape=jax.ShapeDtypeStruct((rows, tokens), BF16),
        grid=(tokens // step_rows,),
        in_specs=[whole(x.shape)],
        out_specs=whole((rows, tokens)),
        scratch_shapes=[
            pltpu.VMEM((columns, tokens), BF16),
            pltpu.VMEM((3 * HEAD_DIM, tokens), BF16),
            pltpu.VMEM((LANES, tokens), BF16),
            pltpu.VMEM((HEAD_DIM, tokens), F32),
            pltpu.VMEM((HEAD_DIM, tokens), F32),
        ],
        compiler_params=pltpu.CompilerParams(vmem_limit_bytes=48 << 20),
        cost_estimate=pl.CostEstimate(
            flops=12 * tokens * tokens * 128, bytes_accessed=4 << 20, transcendentals=tokens * tokens
        ),
        name="attention_gradient",
    )(x)


def exchange(array, axis_name):
    return lax.all_to_all(array, axis_name, split_axis=0, concat_axis=0, tiled=True)


def body(frames, map_weight, qkv_weight, cotangent):
    seq, dp = lax.axis_size("seq"), lax.axis_size("dp")
    columns = qkv_weight.shape[1] // seq
    padded = -(-columns // (16 * dp)) * 16 * dp
    normed, send = learn_tokens(frames[0], map_weight, qkv_weight, cotangent[0], seq)
    tokens = lax.all_gather(normed, "seq", tiled=True)
    grads = attention_gradient(exchange(send, "seq"), padded)
    term = weight_gradient(grads, tokens)
    pieces = exchange(term.reshape(dp, -1, term.shape[1]), "dp")
    summed = jnp.sum(pieces.astype(F32), axis=0).astype(BF16)
    whole = exchange(jnp.broadcast_to(summed[None], (dp,) + summed.shape), "dp")
    return whole.reshape(term.shape)[:columns].astype(F32).T


def solution(mesh):
    placed = (P("dp", "seq", None, None), P(), P(), P("dp", "seq", None))
    return jax.shard_map(
        body, mesh=mesh, in_specs=placed, out_specs=P(None, "seq"), check_vma=False
    )
```

```python
import functools
import math

import jax
import jax.numpy as jnp
from jax import lax
from jax.experimental import pallas as pl
from jax.experimental.pallas import tpu as pltpu
from jax.sharding import PartitionSpec as P

HEAD_DIM = 80
F32, BF16 = jnp.float32, jnp.bfloat16
LANES = 128


def matmul(a, b, dims=((1,), (0,))):
    return lax.dot_general(a, b, (dims, ((), ())), preferred_element_type=F32)


def thirds(value):
    high = value.astype(BF16)
    rest = value - high.astype(F32)
    middle = rest.astype(BF16)
    return high, middle, (rest - middle.astype(F32)).astype(BF16)


def tokens_kernel(group, frames, map_weight, cot, normed, send, held, map_weight_t, cot_held, sems, own_sems):
    count = frames.shape[0]
    slots = map_weight_t.shape[0]
    parts = [pl.ds(g * group, group) for g in range(count // group)]
    loads = [
        pltpu.make_async_copy(frames.at[part], held.at[part], sems.at[g])
        for g, part in enumerate(parts)
    ]
    map_load = pltpu.make_async_copy(map_weight, map_weight_t, own_sems.at[0])
    cot_load = pltpu.make_async_copy(cot, cot_held, own_sems.at[1])
    for load in (map_load, cot_load, *loads):
        load.start()
    map_load.wait()
    cot_load.wait()
    send[...] = cot_held[...].T.reshape(send.shape)
    for g, load in enumerate(loads):
        load.wait()
        blocks = [held[g * group + k] for k in range(group)]
        logits = [matmul(map_weight_t[...], block, ((1,), (1,))) for block in blocks]
        maps = [jax.nn.sigmoid(l).astype(BF16) for l in logits]
        pooled = jnp.concatenate([matmul(m, block) for m, block in zip(maps, blocks)], axis=0)
        centred = pooled - jnp.mean(pooled, axis=-1, keepdims=True)
        variance = jnp.mean(centred * centred, axis=-1, keepdims=True)
        at = g * group * slots
        normed[at : at + group * slots, :] = (centred * lax.rsqrt(variance + 1e-06)).astype(BF16)


def learn_tokens(frames, map_weight, cot, heads):
    count = frames.shape[0]
    tokens, width = cot.shape
    group = math.gcd(count, 4)
    vmem, hbm = pl.BlockSpec(memory_space=pltpu.VMEM), pl.BlockSpec(memory_space=pltpu.HBM)
    return pl.pallas_call(
        functools.partial(tokens_kernel, group),
        out_shape=(
            jax.ShapeDtypeStruct((tokens, width), BF16),
            jax.ShapeDtypeStruct((heads, width // heads, tokens), BF16),
        ),
        in_specs=[hbm, hbm, hbm],
        out_specs=(vmem, vmem),
        scratch_shapes=[
            pltpu.VMEM(frames.shape, BF16),
            pltpu.VMEM(map_weight.shape[::-1], BF16),
            pltpu.VMEM(cot.shape, BF16),
            pltpu.SemaphoreType.DMA((count // group,)),
            pltpu.SemaphoreType.DMA((2,)),
        ],
        compiler_params=pltpu.CompilerParams(vmem_limit_bytes=62 << 20),
        name="learn_tokens",
    )(frames, map_weight.T, cot)


def head_kernel(sub, order_ref, cot_ref, weight_ref, *refs):
    pieces = cot_ref.shape[0]
    chunks, out_ref = refs[:pieces], refs[pieces]
    x, k3, v1, grads, query_scaled, cot_scaled, shifted_all, scores_all = refs[pieces + 1 :]
    hd = HEAD_DIM
    scale = 1.0 / math.sqrt(hd)
    width = cot_ref.shape[2]
    count = pieces * width
    join = 4
    for at in range(0, pieces, join):
        tokens = jnp.concatenate([chunk[...] for chunk in chunks[at : at + join]], axis=0)
        columns = slice(at * width, (at + join) * width)
        x[0 : 3 * hd, columns] = matmul(tokens, weight_ref[...]).T.astype(BF16)
    for piece in range(pieces):
        x[3 * hd :, piece * width : (piece + 1) * width] = cot_ref[order_ref[piece]]
    key = x[hd : 2 * hd, :]
    k3[...] = jnp.concatenate([key, key, key], axis=0)
    row = lax.broadcasted_iota(jnp.int32, (LANES - hd, count), 0)
    ones = jnp.where(row < 3, 1.0, 0.0).astype(BF16)
    v1[...] = jnp.concatenate([x[2 * hd : 3 * hd, :], ones], axis=0)
    lane = lax.broadcasted_iota(jnp.int32, (sub, LANES - hd), 1)
    blocks = count // sub
    state = [{} for _ in range(blocks)]

    def rows(s):
        return slice(s * sub, (s + 1) * sub)

    def score(s):
        query = x[0:hd, rows(s)].astype(F32)
        terms = jnp.concatenate(thirds(query * (scale * math.log2(math.e))), axis=0).T
        state[s].update(query=query, scores=matmul(terms, k3[...]))

    def exponent(s):
        scores = state[s].pop("scores")
        shifted = jnp.exp2(scores - jnp.max(scores, axis=-1, keepdims=True)).astype(BF16)
        shifted_all[rows(s), :] = shifted
        state[s]["shifted"] = shifted

    def attend(s):
        cot_t = x[3 * hd :, rows(s)]
        cot = cot_t.T
        attended = matmul(state[s]["shifted"], v1[...], ((1,), (1,)))
        inverse = 1.0 / attended[:, hd : hd + 1]
        row_dot = jnp.sum(cot.astype(F32) * attended[:, 0:hd], axis=-1, keepdims=True) * inverse
        first, second, third = (t.astype(F32) for t in thirds(-row_dot))
        tail = jnp.where(
            lane == 0, first, jnp.where(lane == 1, second, jnp.where(lane == 2, third, 0.0))
        ).astype(BF16)
        difference = matmul(jnp.concatenate([cot, tail], axis=1), v1[...])
        state[s].update(cot_t=cot_t, inverse=inverse, difference=difference)

    def grad_score(s):
        grad_scores = (state[s]["shifted"].astype(F32) * state[s].pop("difference")).astype(BF16)
        scores_all[rows(s), :] = grad_scores
        state[s]["grad_scores"] = grad_scores

    def grad_query(s):
        inverse = state[s]["inverse"]
        product = matmul(state[s]["grad_scores"], k3[0:hd, :], ((1,), (1,))) * (inverse * scale)
        grads[0:hd, rows(s)] = product.T.astype(BF16)
        inverse_t = jnp.broadcast_to(inverse, (sub, LANES)).T[0:1, :]
        query_scaled[:, rows(s)] = (state[s]["query"] * (inverse_t * scale)).astype(BF16)
        cot_scaled[:, rows(s)] = (state[s]["cot_t"].astype(F32) * inverse_t).astype(BF16)
        state[s].clear()

    def both(stage, pair):
        for s in (2 * pair, 2 * pair + 1):
            if s < blocks:
                stage(s)

    both(score, 0)
    both(exponent, 0)
    for pair in range(blocks // 2):
        both(score, pair + 1)
        both(attend, pair)
        both(exponent, pair + 1)
        both(grad_score, pair)
        both(grad_query, pair)
    grads[hd : 2 * hd, :] = matmul(query_scaled[...], scores_all[...]).astype(BF16)
    grads[2 * hd : 3 * hd, :] = matmul(cot_scaled[...], shifted_all[...]).astype(BF16)
    grads[3 * hd :, :] = jnp.zeros((grads.shape[0] - 3 * hd, count), BF16)
    total = None
    for at in range(0, pieces, join):
        tokens = jnp.concatenate([chunk[...] for chunk in chunks[at : at + join]], axis=0)
        term = matmul(grads[:, at * width : (at + join) * width], tokens)
        total = term if total is None else total + term
    out_ref[...] = total.astype(BF16)


def head_gradient(order, cot, weight, chunks, rows):
    pieces, _, width = cot.shape
    count = pieces * width
    vmem = pl.BlockSpec(memory_space=pltpu.VMEM)
    return pl.pallas_call(
        functools.partial(head_kernel, 256),
        out_shape=jax.ShapeDtypeStruct((rows, chunks[0].shape[1]), BF16),
        in_specs=[pl.BlockSpec(memory_space=pltpu.SMEM)] + [vmem] * (2 + pieces),
        out_specs=vmem,
        scratch_shapes=[
            pltpu.VMEM((4 * HEAD_DIM, count), BF16),
            pltpu.VMEM((3 * HEAD_DIM, count), BF16),
            pltpu.VMEM((LANES, count), BF16),
            pltpu.VMEM((rows, count), BF16),
            pltpu.VMEM((HEAD_DIM, count), BF16),
            pltpu.VMEM((HEAD_DIM, count), BF16),
            pltpu.VMEM((count, count), BF16),
            pltpu.VMEM((count, count), BF16),
        ],
        compiler_params=pltpu.CompilerParams(vmem_limit_bytes=52 << 20),
        cost_estimate=pl.CostEstimate(
            flops=12 * count * count * LANES, bytes_accessed=8 << 20, transcendentals=count * count
        ),
        name="head_gradient",
    )(order, cot, weight, *chunks)


def exchange(array, axis_name):
    return lax.all_to_all(array, axis_name, split_axis=0, concat_axis=0, tiled=True)


RING, CORES = 4, 2


def gather_pieces(own):
    count = lax.axis_size("seq")
    me = lax.axis_index("seq")

    def over(index, dz, dx, dc):
        plane, x, core = index // (RING * CORES), index // CORES % RING, index % CORES
        return (plane ^ dz) * RING * CORES + (x + dx) % RING * CORES + (core ^ dc)

    def send(array, *by):
        return lax.ppermute(array, "seq", [(i, over(i, *by)) for i in range(count)])

    right, left = send(own, 0, 1, 0), send(own, 0, -1, 0)
    other = send(own, 1, 0, 0)
    other_right, other_left = send(other, 0, 1, 0), send(other, 0, -1, 0)
    across, other_across = send(right, 0, 1, 0), send(other_left, 0, -1, 0)
    near = [own, other, right, left, other_right, other_left, across, other_across]
    places = [(0, 0), (1, 0), (0, -1), (0, 1), (1, -1), (1, 1), (0, -2), (1, 2)]
    pieces, order = list(near), [over(me, dz, dx, 0) for dz, dx in places]
    for array, (dz, dx) in zip(near, places):
        pieces.append(send(array, 0, 0, 1))
        order.append(over(me, dz, dx, 1))
    return pieces, jnp.stack(order).astype(jnp.int32)


def body(frames, map_weight, qkv_weight, cotangent):
    seq, dp = lax.axis_size("seq"), lax.axis_size("dp")
    columns = qkv_weight.shape[1] // seq
    padded = -(-columns // (16 * dp)) * 16 * dp
    normed, send = learn_tokens(frames[0], map_weight, cotangent[0], seq)
    pieces, order = gather_pieces(normed)
    own_weight = lax.dynamic_slice_in_dim(qkv_weight, lax.axis_index("seq") * columns, columns, 1)
    term = head_gradient(order, exchange(send, "seq"), own_weight, pieces, padded)
    parts = exchange(term.reshape(dp, -1, term.shape[1]), "dp")
    summed = jnp.sum(parts.astype(F32), axis=0).astype(BF16)
    whole = exchange(jnp.broadcast_to(summed[None], (dp,) + summed.shape), "dp")
    return whole.reshape(term.shape)[:columns].astype(F32).T


def solution(mesh):
    placed = (P("dp", "seq", None, None), P(), P(), P("dp", "seq", None))
    return jax.shard_map(
        body, mesh=mesh, in_specs=placed, out_specs=P(None, "seq"), check_vma=False
    )
```

```python
import functools
import math

import jax
import jax.numpy as jnp
from jax import lax
from jax.experimental import pallas as pl
from jax.experimental.pallas import tpu as pltpu
from jax.sharding import PartitionSpec as P

HEAD_DIM = 80
F32, BF16 = jnp.float32, jnp.bfloat16
LANES = 128


def matmul(a, b, dims=((1,), (0,))):
    return lax.dot_general(a, b, (dims, ((), ())), preferred_element_type=F32)


def thirds(value):
    high = value.astype(BF16)
    rest = value - high.astype(F32)
    middle = rest.astype(BF16)
    return high, middle, (rest - middle.astype(F32)).astype(BF16)


def tokens_kernel(
    group, ahead, frames, map_weight, cot, normed, send, held, map_weight_t, cot_held, pooled, sems, own_sems
):
    count = frames.shape[0]
    slots = map_weight_t.shape[0]
    step = count // sems.shape[0]
    parts = [pl.ds(i * step, step) for i in range(sems.shape[0])]
    loads = [
        pltpu.make_async_copy(frames.at[part], held.at[part], sems.at[i])
        for i, part in enumerate(parts)
    ]
    map_load = pltpu.make_async_copy(map_weight, map_weight_t, own_sems.at[0])
    cot_load = pltpu.make_async_copy(cot, cot_held, own_sems.at[1])
    map_load.start()
    waiting = loads + [cot_load]
    for load in waiting[:ahead]:
        load.start()
    waiting = waiting[ahead:]
    map_load.wait()
    for g in range(count // group):
        for load in loads[g * group // step : (g + 1) * group // step]:
            load.wait()
            if waiting:
                waiting.pop(0).start()
        blocks = [held[g * group + k] for k in range(group)]
        logits = [matmul(map_weight_t[...], block, ((1,), (1,))) for block in blocks]
        maps = [jax.nn.sigmoid(l).astype(BF16) for l in logits]
        at = g * group * slots
        pooled[at : at + group * slots, :] = jnp.concatenate(
            [matmul(m, block) for m, block in zip(maps, blocks)], axis=0
        )
    for load in waiting:
        load.start()
    centred = pooled[...] - jnp.mean(pooled[...], axis=-1, keepdims=True)
    variance = jnp.mean(centred * centred, axis=-1, keepdims=True)
    normed[...] = (centred * lax.rsqrt(variance + 1e-06)).astype(BF16)
    cot_load.wait()
    send[...] = cot_held[...].T.reshape(send.shape)


def learn_tokens(frames, map_weight, cot, heads):
    count = frames.shape[0]
    tokens, width = cot.shape
    vmem, hbm = pl.BlockSpec(memory_space=pltpu.VMEM), pl.BlockSpec(memory_space=pltpu.HBM)
    return pl.pallas_call(
        functools.partial(tokens_kernel, math.gcd(count, 4), 4),
        out_shape=(
            jax.ShapeDtypeStruct((tokens, width), BF16),
            jax.ShapeDtypeStruct((heads, width // heads, tokens), BF16),
        ),
        in_specs=[hbm, hbm, hbm],
        out_specs=(vmem, vmem),
        scratch_shapes=[
            pltpu.VMEM(frames.shape, BF16),
            pltpu.VMEM(map_weight.shape[::-1], BF16),
            pltpu.VMEM(cot.shape, BF16),
            pltpu.VMEM(cot.shape, F32),
            pltpu.SemaphoreType.DMA((count // math.gcd(count, 2),)),
            pltpu.SemaphoreType.DMA((2,)),
        ],
        compiler_params=pltpu.CompilerParams(vmem_limit_bytes=62 << 20),
        name="learn_tokens",
    )(frames, map_weight.T, cot)


def head_kernel(sub, order_ref, cot_ref, weight_ref, *refs):
    pieces = cot_ref.shape[0]
    chunks, out_ref = refs[:pieces], refs[pieces]
    held, sems, x, k3, v1, grads, query_scaled, cot_scaled, shifted_all, scores_all = refs[pieces + 1 :]
    hd = HEAD_DIM
    scale = 1.0 / math.sqrt(hd)
    width = cot_ref.shape[2]
    count = pieces * width
    join = 4
    loads = [
        pltpu.make_async_copy(chunk, held.at[pl.ds(i * width, width)], sems.at[i])
        for i, chunk in enumerate(chunks)
    ]
    for load in loads:
        load.start()
    for piece in range(pieces):
        x[3 * hd :, piece * width : (piece + 1) * width] = cot_ref[order_ref[piece]]
    for at in range(0, pieces, join):
        for load in loads[at : at + join]:
            load.wait()
        columns = slice(at * width, (at + join) * width)
        x[0 : 3 * hd, columns] = matmul(held[columns, :], weight_ref[...]).T.astype(BF16)
    key = x[hd : 2 * hd, :]
    k3[...] = jnp.concatenate([key, key, key], axis=0)
    row = lax.broadcasted_iota(jnp.int32, (LANES - hd, count), 0)
    ones = jnp.where(row < 3, 1.0, 0.0).astype(BF16)
    v1[...] = jnp.concatenate([x[2 * hd : 3 * hd, :], ones], axis=0)
    lane = lax.broadcasted_iota(jnp.int32, (sub, LANES - hd), 1)
    blocks = count // sub
    state = [{} for _ in range(blocks)]

    def rows(s):
        return slice(s * sub, (s + 1) * sub)

    def score(s):
        query = x[0:hd, rows(s)].astype(F32)
        terms = jnp.concatenate(thirds(query * (scale * math.log2(math.e))), axis=0).T
        state[s].update(query=query, scores=matmul(terms, k3[...]))

    def exponent(s):
        scores = state[s].pop("scores")
        shifted = jnp.exp2(scores - jnp.max(scores, axis=-1, keepdims=True)).astype(BF16)
        shifted_all[rows(s), :] = shifted
        state[s]["shifted"] = shifted

    def attend(s):
        cot_t = x[3 * hd :, rows(s)]
        cot = cot_t.T
        attended = matmul(state[s]["shifted"], v1[...], ((1,), (1,)))
        inverse = 1.0 / attended[:, hd : hd + 1]
        row_dot = jnp.sum(cot.astype(F32) * attended[:, 0:hd], axis=-1, keepdims=True) * inverse
        first, second, third = (t.astype(F32) for t in thirds(-row_dot))
        tail = jnp.where(
            lane == 0, first, jnp.where(lane == 1, second, jnp.where(lane == 2, third, 0.0))
        ).astype(BF16)
        difference = matmul(jnp.concatenate([cot, tail], axis=1), v1[...])
        state[s].update(cot_t=cot_t, inverse=inverse, difference=difference)

    def grad_score(s):
        grad_scores = (state[s]["shifted"].astype(F32) * state[s].pop("difference")).astype(BF16)
        scores_all[rows(s), :] = grad_scores
        state[s]["grad_scores"] = grad_scores

    def grad_query(s):
        inverse = state[s]["inverse"]
        product = matmul(state[s]["grad_scores"], k3[0:hd, :], ((1,), (1,))) * (inverse * scale)
        grads[0:hd, rows(s)] = product.T.astype(BF16)
        inverse_t = jnp.broadcast_to(inverse, (sub, LANES)).T[0:1, :]
        query_scaled[:, rows(s)] = (state[s]["query"] * (inverse_t * scale)).astype(BF16)
        cot_scaled[:, rows(s)] = (state[s]["cot_t"].astype(F32) * inverse_t).astype(BF16)
        state[s].clear()

    def both(stage, pair):
        for s in (2 * pair, 2 * pair + 1):
            if s < blocks:
                stage(s)

    both(score, 0)
    both(exponent, 0)
    for pair in range(blocks // 2):
        both(score, pair + 1)
        both(attend, pair)
        both(exponent, pair + 1)
        both(grad_score, pair)
        both(grad_query, pair)
    grads[hd : 2 * hd, :] = matmul(query_scaled[...], scores_all[...]).astype(BF16)
    grads[2 * hd : 3 * hd, :] = matmul(cot_scaled[...], shifted_all[...]).astype(BF16)
    grads[3 * hd :, :] = jnp.zeros((grads.shape[0] - 3 * hd, count), BF16)
    out_ref[...] = matmul(grads[...], held[...]).astype(BF16)


def head_gradient(order, cot, weight, chunks, rows):
    pieces, _, width = cot.shape
    count = pieces * width
    vmem = pl.BlockSpec(memory_space=pltpu.VMEM)
    return pl.pallas_call(
        functools.partial(head_kernel, 256),
        out_shape=jax.ShapeDtypeStruct((rows, chunks[0].shape[1]), BF16),
        in_specs=[pl.BlockSpec(memory_space=pltpu.SMEM)] + [vmem] * 2 + [pl.BlockSpec(memory_space=pl.ANY)] * pieces,
        out_specs=vmem,
        scratch_shapes=[
            pltpu.VMEM((count, chunks[0].shape[1]), BF16),
            pltpu.SemaphoreType.DMA((pieces,)),
            pltpu.VMEM((4 * HEAD_DIM, count), BF16),
            pltpu.VMEM((3 * HEAD_DIM, count), BF16),
            pltpu.VMEM((LANES, count), BF16),
            pltpu.VMEM((rows, count), BF16),
            pltpu.VMEM((HEAD_DIM, count), BF16),
            pltpu.VMEM((HEAD_DIM, count), BF16),
            pltpu.VMEM((count, count), BF16),
            pltpu.VMEM((count, count), BF16),
        ],
        compiler_params=pltpu.CompilerParams(vmem_limit_bytes=48 << 20),
        cost_estimate=pl.CostEstimate(
            flops=12 * count * count * LANES, bytes_accessed=8 << 20, transcendentals=count * count
        ),
        name="head_gradient",
    )(order, cot, weight, *chunks)


def exchange(array, axis_name):
    return lax.all_to_all(array, axis_name, split_axis=0, concat_axis=0, tiled=True)


RING, CORES = 4, 2


def gather_pieces(own, weight, cot):
    count = lax.axis_size("seq")
    me = lax.axis_index("seq")

    def over(index, dz, dx, dc):
        plane, x, core = index // (RING * CORES), index // CORES % RING, index % CORES
        return (plane ^ dz) * RING * CORES + (x + dx) % RING * CORES + (core ^ dc)

    def send(array, *by):
        return lax.ppermute(array, "seq", [(i, over(i, *by)) for i in range(count)])

    right, left = send(own, 0, 1, 0), send(own, 0, -1, 0)
    other = send(own, 1, 0, 0)
    other_right, other_left = send(other, 0, 1, 0), send(other, 0, -1, 0)
    right, weight = lax.optimization_barrier((right, weight))
    across, other_across = send(right, 0, 1, 0), send(other_left, 0, -1, 0)
    across, cot = lax.optimization_barrier((across, exchange(cot, "seq")))
    near = [own, other, right, left, other_right, other_left, across, other_across]
    places = [(0, 0), (1, 0), (0, -1), (0, 1), (1, -1), (1, 1), (0, -2), (1, 2)]
    pieces, order = list(near), [over(me, dz, dx, 0) for dz, dx in places]
    for array, (dz, dx) in zip(near, places):
        pieces.append(send(array, 0, 0, 1))
        order.append(over(me, dz, dx, 1))
    return pieces, jnp.stack(order).astype(jnp.int32), weight, cot


def body(frames, map_weight, qkv_weight, cotangent):
    seq, dp = lax.axis_size("seq"), lax.axis_size("dp")
    columns = qkv_weight.shape[1] // seq
    padded = -(-columns // (16 * dp)) * 16 * dp
    normed, send = learn_tokens(frames[0], map_weight, cotangent[0], seq)
    own_weight = lax.dynamic_slice_in_dim(qkv_weight, lax.axis_index("seq") * columns, columns, 1)
    pieces, order, own_weight, cot = gather_pieces(normed, own_weight, send)
    term = head_gradient(order, cot, own_weight, pieces, padded)
    parts = exchange(term.reshape(dp, -1, term.shape[1]), "dp")
    summed = jnp.sum(parts.astype(F32), axis=0).astype(BF16)
    whole = exchange(jnp.broadcast_to(summed[None], (dp,) + summed.shape), "dp")
    return whole.reshape(term.shape)[:columns].astype(F32).T


def solution(mesh):
    placed = (P("dp", "seq", None, None), P(), P(), P("dp", "seq", None))
    return jax.shard_map(
        body, mesh=mesh, in_specs=placed, out_specs=P(None, "seq"), check_vma=False
    )
```

```python
import functools
import math

import jax
import jax.numpy as jnp
from jax import lax
from jax.experimental import pallas as pl
from jax.experimental.pallas import tpu as pltpu
from jax.sharding import PartitionSpec as P

HEAD_DIM = 80
F32, BF16 = jnp.float32, jnp.bfloat16
LANES = 128


def matmul(a, b, dims=((1,), (0,))):
    return lax.dot_general(a, b, (dims, ((), ())), preferred_element_type=F32)


def thirds(value):
    high = value.astype(BF16)
    rest = value - high.astype(F32)
    middle = rest.astype(BF16)
    return high, middle, (rest - middle.astype(F32)).astype(BF16)


def tokens_kernel(
    group, ahead, frames, map_weight, cot, normed, send, held, map_weight_t, cot_held, pooled, sems, own_sems
):
    count = frames.shape[0]
    slots = map_weight_t.shape[0]
    step = count // sems.shape[0]
    parts = [pl.ds(i * step, step) for i in range(sems.shape[0])]
    loads = [
        pltpu.make_async_copy(frames.at[part], held.at[part], sems.at[i])
        for i, part in enumerate(parts)
    ]
    map_load = pltpu.make_async_copy(map_weight, map_weight_t, own_sems.at[0])
    cot_load = pltpu.make_async_copy(cot, cot_held, own_sems.at[1])
    map_load.start()
    waiting = loads + [cot_load]
    for load in waiting[:ahead]:
        load.start()
    waiting = waiting[ahead:]
    map_load.wait()
    for g in range(count // group):
        for load in loads[g * group // step : (g + 1) * group // step]:
            load.wait()
            if waiting:
                waiting.pop(0).start()
        blocks = [held[g * group + k] for k in range(group)]
        logits = [matmul(map_weight_t[...], block, ((1,), (1,))) for block in blocks]
        maps = [jax.nn.sigmoid(l).astype(BF16) for l in logits]
        at = g * group * slots
        pooled[at : at + group * slots, :] = jnp.concatenate(
            [matmul(m, block) for m, block in zip(maps, blocks)], axis=0
        )
    for load in waiting:
        load.start()
    centred = pooled[...] - jnp.mean(pooled[...], axis=-1, keepdims=True)
    variance = jnp.mean(centred * centred, axis=-1, keepdims=True)
    normed[...] = (centred * lax.rsqrt(variance + 1e-06)).astype(BF16)
    cot_load.wait()
    send[...] = cot_held[...].T.reshape(send.shape)


def learn_tokens(frames, map_weight, cot, heads):
    count = frames.shape[0]
    tokens, width = cot.shape
    vmem, hbm = pl.BlockSpec(memory_space=pltpu.VMEM), pl.BlockSpec(memory_space=pltpu.HBM)
    return pl.pallas_call(
        functools.partial(tokens_kernel, math.gcd(count, 4), 4),
        out_shape=(
            jax.ShapeDtypeStruct((tokens, width), BF16),
            jax.ShapeDtypeStruct((heads, width // heads, tokens), BF16),
        ),
        in_specs=[hbm, hbm, hbm],
        out_specs=(vmem, vmem),
        scratch_shapes=[
            pltpu.VMEM(frames.shape, BF16),
            pltpu.VMEM(map_weight.shape[::-1], BF16),
            pltpu.VMEM(cot.shape, BF16),
            pltpu.VMEM(cot.shape, F32),
            pltpu.SemaphoreType.DMA((count // math.gcd(count, 2),)),
            pltpu.SemaphoreType.DMA((2,)),
        ],
        compiler_params=pltpu.CompilerParams(vmem_limit_bytes=62 << 20),
        name="learn_tokens",
    )(frames, map_weight.T, cot)


def head_kernel(sub, order_ref, cot_ref, weight_ref, *refs):
    pieces = cot_ref.shape[0]
    chunks, out_ref = refs[:pieces], refs[pieces]
    x, k3, v1, grads, query_scaled, cot_scaled, shifted_all, scores_all = refs[pieces + 1 :]
    hd = HEAD_DIM
    scale = 1.0 / math.sqrt(hd)
    width = cot_ref.shape[2]
    count = pieces * width
    join = 4
    for piece in range(pieces):
        x[3 * hd :, piece * width : (piece + 1) * width] = cot_ref[order_ref[piece]]
    weight_t = weight_ref[...].T
    for at in range(0, pieces, join):
        tokens = jnp.concatenate([chunk[...] for chunk in chunks[at : at + join]], axis=0)
        columns = slice(at * width, (at + join) * width)
        x[0 : 3 * hd, columns] = matmul(weight_t, tokens, ((1,), (1,))).astype(BF16)
    key = x[hd : 2 * hd, :]
    k3[...] = jnp.concatenate([key, key, key], axis=0)
    row = lax.broadcasted_iota(jnp.int32, (LANES - hd, count), 0)
    ones = jnp.where(row < 3, 1.0, 0.0).astype(BF16)
    v1[...] = jnp.concatenate([x[2 * hd : 3 * hd, :], ones], axis=0)
    lane = lax.broadcasted_iota(jnp.int32, (sub, LANES - hd), 1)
    blocks = count // sub
    state = [{} for _ in range(blocks)]

    def rows(s):
        return slice(s * sub, (s + 1) * sub)

    def score(s):
        query = x[0:hd, rows(s)].astype(F32)
        terms = jnp.concatenate(thirds(query * (scale * math.log2(math.e))), axis=0).T
        state[s].update(query=query, scores=matmul(terms, k3[...]))

    def exponent(s):
        scores = state[s].pop("scores")
        shifted = jnp.exp2(scores - jnp.max(scores, axis=-1, keepdims=True)).astype(BF16)
        shifted_all[rows(s), :] = shifted
        state[s]["shifted"] = shifted

    def attend(s):
        cot_t = x[3 * hd :, rows(s)]
        cot = cot_t.T
        attended = matmul(state[s]["shifted"], v1[...], ((1,), (1,)))
        inverse = 1.0 / attended[:, hd : hd + 1]
        row_dot = jnp.sum(cot.astype(F32) * attended[:, 0:hd], axis=-1, keepdims=True) * inverse
        first, second, third = (t.astype(F32) for t in thirds(-row_dot))
        tail = jnp.where(
            lane == 0, first, jnp.where(lane == 1, second, jnp.where(lane == 2, third, 0.0))
        ).astype(BF16)
        difference = matmul(jnp.concatenate([cot, tail], axis=1), v1[...])
        state[s].update(cot_t=cot_t, inverse=inverse, difference=difference)

    def grad_score(s):
        grad_scores = (state[s]["shifted"].astype(F32) * state[s].pop("difference")).astype(BF16)
        scores_all[rows(s), :] = grad_scores
        state[s]["grad_scores"] = grad_scores

    def grad_query(s):
        inverse = state[s]["inverse"]
        product = matmul(state[s]["grad_scores"], k3[0:hd, :], ((1,), (1,))) * (inverse * scale)
        grads[0:hd, rows(s)] = product.T.astype(BF16)
        inverse_t = jnp.broadcast_to(inverse, (sub, LANES)).T[0:1, :]
        query_scaled[:, rows(s)] = (state[s]["query"] * (inverse_t * scale)).astype(BF16)
        cot_scaled[:, rows(s)] = (state[s]["cot_t"].astype(F32) * inverse_t).astype(BF16)
        state[s].clear()

    def both(stage, pair):
        for s in (2 * pair, 2 * pair + 1):
            if s < blocks:
                stage(s)

    both(score, 0)
    both(exponent, 0)
    for pair in range(blocks // 2):
        both(score, pair + 1)
        both(attend, pair)
        both(exponent, pair + 1)
        both(grad_score, pair)
        both(grad_query, pair)
    grads[hd : 2 * hd, :] = matmul(query_scaled[...], scores_all[...]).astype(BF16)
    grads[2 * hd : 3 * hd, :] = matmul(cot_scaled[...], shifted_all[...]).astype(BF16)
    grads[3 * hd :, :] = jnp.zeros((grads.shape[0] - 3 * hd, count), BF16)
    total = None
    for at in range(0, pieces, join):
        tokens = jnp.concatenate([chunk[...] for chunk in chunks[at : at + join]], axis=0)
        term = matmul(grads[:, at * width : (at + join) * width], tokens)
        total = term if total is None else total + term
    out_ref[...] = total.astype(BF16)


def head_gradient(order, cot, weight, chunks, rows):
    pieces, _, width = cot.shape
    count = pieces * width
    vmem = pl.BlockSpec(memory_space=pltpu.VMEM)
    return pl.pallas_call(
        functools.partial(head_kernel, 256),
        out_shape=jax.ShapeDtypeStruct((rows, chunks[0].shape[1]), BF16),
        in_specs=[pl.BlockSpec(memory_space=pltpu.SMEM)] + [vmem] * (2 + pieces),
        out_specs=vmem,
        scratch_shapes=[
            pltpu.VMEM((4 * HEAD_DIM, count), BF16),
            pltpu.VMEM((3 * HEAD_DIM, count), BF16),
            pltpu.VMEM((LANES, count), BF16),
            pltpu.VMEM((rows, count), BF16),
            pltpu.VMEM((HEAD_DIM, count), BF16),
            pltpu.VMEM((HEAD_DIM, count), BF16),
            pltpu.VMEM((count, count), BF16),
            pltpu.VMEM((count, count), BF16),
        ],
        compiler_params=pltpu.CompilerParams(vmem_limit_bytes=42 << 20),
        cost_estimate=pl.CostEstimate(
            flops=12 * count * count * LANES, bytes_accessed=8 << 20, transcendentals=count * count
        ),
        name="head_gradient",
    )(order, cot, weight, *chunks)


def exchange(array, axis_name):
    return lax.all_to_all(array, axis_name, split_axis=0, concat_axis=0, tiled=True)


RING, CORES = 4, 2


def gather_pieces(own, weight, cot):
    count = lax.axis_size("seq")
    me = lax.axis_index("seq")

    def over(index, dz, dx, dc):
        plane, x, core = index // (RING * CORES), index // CORES % RING, index % CORES
        return (plane ^ dz) * RING * CORES + (x + dx) % RING * CORES + (core ^ dc)

    def send(array, *by):
        return lax.ppermute(array, "seq", [(i, over(i, *by)) for i in range(count)])

    right, left = send(own, 0, 1, 0), send(own, 0, -1, 0)
    other = send(own, 1, 0, 0)
    other_right, other_left = send(other, 0, 1, 0), send(other, 0, -1, 0)
    right, weight = lax.optimization_barrier((right, weight))
    across, other_across = send(right, 0, 1, 0), send(other_left, 0, -1, 0)
    across, cot = lax.optimization_barrier((across, exchange(cot, "seq")))
    near = [own, other, right, left, other_right, other_left, across, other_across]
    places = [(0, 0), (1, 0), (0, -1), (0, 1), (1, -1), (1, 1), (0, -2), (1, 2)]
    pieces, order = list(near), [over(me, dz, dx, 0) for dz, dx in places]
    for array, (dz, dx) in zip(near, places):
        pieces.append(send(array, 0, 0, 1))
        order.append(over(me, dz, dx, 1))
    return pieces, jnp.stack(order).astype(jnp.int32), weight, cot


def body(frames, map_weight, qkv_weight, cotangent):
    seq, dp = lax.axis_size("seq"), lax.axis_size("dp")
    columns = qkv_weight.shape[1] // seq
    padded = -(-columns // (16 * dp)) * 16 * dp
    normed, send = learn_tokens(frames[0], map_weight, cotangent[0], seq)
    own_weight = lax.dynamic_slice_in_dim(qkv_weight, lax.axis_index("seq") * columns, columns, 1)
    pieces, order, own_weight, cot = gather_pieces(normed, own_weight, send)
    term = head_gradient(order, cot, own_weight, pieces, padded)
    parts = exchange(term.reshape(dp, -1, term.shape[1]), "dp")
    summed = jnp.sum(parts.astype(F32), axis=0).astype(BF16)
    whole = exchange(jnp.broadcast_to(summed[None], (dp,) + summed.shape), "dp")
    return whole.reshape(term.shape)[:columns].astype(F32).T


def solution(mesh):
    placed = (P("dp", "seq", None, None), P(), P(), P("dp", "seq", None))
    return jax.shard_map(
        body, mesh=mesh, in_specs=placed, out_specs=P(None, "seq"), check_vma=False
    )
```

```python
import functools
import math

import jax
import jax.numpy as jnp
from jax import lax
from jax.experimental import pallas as pl
from jax.experimental.pallas import tpu as pltpu
from jax.sharding import PartitionSpec as P

HEAD_DIM = 80
F32, BF16 = jnp.float32, jnp.bfloat16
LANES = 128


def matmul(a, b, dims=((1,), (0,))):
    return lax.dot_general(a, b, (dims, ((), ())), preferred_element_type=F32)


def thirds(value):
    high = value.astype(BF16)
    rest = value - high.astype(F32)
    middle = rest.astype(BF16)
    return high, middle, (rest - middle.astype(F32)).astype(BF16)


def tokens_kernel(
    group, ahead, frames, map_weight, cot, normed, send, held, map_weight_t, cot_held, pooled, sems, own_sems
):
    count = frames.shape[0]
    slots = map_weight_t.shape[0]
    step = count // sems.shape[0]
    parts = [pl.ds(i * step, step) for i in range(sems.shape[0])]
    loads = [
        pltpu.make_async_copy(frames.at[part], held.at[part], sems.at[i])
        for i, part in enumerate(parts)
    ]
    map_load = pltpu.make_async_copy(map_weight, map_weight_t, own_sems.at[0])
    cot_load = pltpu.make_async_copy(cot, cot_held, own_sems.at[1])
    map_load.start()
    waiting = loads + [cot_load]
    for load in waiting[:ahead]:
        load.start()
    waiting = waiting[ahead:]
    map_load.wait()
    for g in range(count // group):
        for load in loads[g * group // step : (g + 1) * group // step]:
            load.wait()
            if waiting:
                waiting.pop(0).start()
        blocks = [held[g * group + k] for k in range(group)]
        logits = [matmul(map_weight_t[...], block, ((1,), (1,))) for block in blocks]
        maps = [jax.nn.sigmoid(l).astype(BF16) for l in logits]
        at = g * group * slots
        pooled[at : at + group * slots, :] = jnp.concatenate(
            [matmul(m, block) for m, block in zip(maps, blocks)], axis=0
        )
    for load in waiting:
        load.start()
    centred = pooled[...] - jnp.mean(pooled[...], axis=-1, keepdims=True)
    variance = jnp.mean(centred * centred, axis=-1, keepdims=True)
    normed[...] = (centred * lax.rsqrt(variance + 1e-06)).astype(BF16)
    cot_load.wait()
    send[...] = cot_held[...].T.reshape(send.shape)


def learn_tokens(frames, map_weight, cot, heads):
    count = frames.shape[0]
    tokens, width = cot.shape
    vmem, hbm = pl.BlockSpec(memory_space=pltpu.VMEM), pl.BlockSpec(memory_space=pltpu.HBM)
    return pl.pallas_call(
        functools.partial(tokens_kernel, math.gcd(count, 4), 4),
        out_shape=(
            jax.ShapeDtypeStruct((tokens, width), BF16),
            jax.ShapeDtypeStruct((heads, width // heads, tokens), BF16),
        ),
        in_specs=[hbm, hbm, hbm],
        out_specs=(vmem, vmem),
        scratch_shapes=[
            pltpu.VMEM(frames.shape, BF16),
            pltpu.VMEM(map_weight.shape[::-1], BF16),
            pltpu.VMEM(cot.shape, BF16),
            pltpu.VMEM(cot.shape, F32),
            pltpu.SemaphoreType.DMA((count // math.gcd(count, 2),)),
            pltpu.SemaphoreType.DMA((2,)),
        ],
        compiler_params=pltpu.CompilerParams(vmem_limit_bytes=62 << 20),
        name="learn_tokens",
    )(frames, map_weight.T, cot)


def head_kernel(sub, order_ref, cot_ref, weight_ref, *refs):
    pieces = cot_ref.shape[0]
    chunks, out_ref = refs[:pieces], refs[pieces]
    x, k3, v1, grads, query_scaled, cot_scaled, shifted_all, scores_all = refs[pieces + 1 :]
    hd = HEAD_DIM
    scale = 1.0 / math.sqrt(hd)
    width = cot_ref.shape[2]
    count = pieces * width
    join = 4
    for piece in range(pieces):
        x[3 * hd :, piece * width : (piece + 1) * width] = cot_ref[order_ref[piece]]
    weight_t = weight_ref[...].T
    for at in range(0, pieces, join):
        tokens = jnp.concatenate([chunk[...] for chunk in chunks[at : at + join]], axis=0)
        columns = slice(at * width, (at + join) * width)
        x[0 : 3 * hd, columns] = matmul(weight_t, tokens, ((1,), (1,))).astype(BF16)
    key = x[hd : 2 * hd, :]
    k3[...] = jnp.concatenate([key, key, key], axis=0)
    row = lax.broadcasted_iota(jnp.int32, (LANES - hd, count), 0)
    ones = jnp.where(row < 3, 1.0, 0.0).astype(BF16)
    v1[...] = jnp.concatenate([x[2 * hd : 3 * hd, :], ones], axis=0)
    lane = lax.broadcasted_iota(jnp.int32, (sub, LANES - hd), 1)
    blocks = count // sub
    state = [{} for _ in range(blocks)]

    def rows(s):
        return slice(s * sub, (s + 1) * sub)

    def score(s):
        query = x[0:hd, rows(s)].astype(F32)
        terms = jnp.concatenate(thirds(query * (scale * math.log2(math.e))), axis=0).T
        state[s].update(query=query, scores=matmul(terms, k3[...]))

    def exponent(s):
        scores = state[s].pop("scores")
        shifted = jnp.exp2(scores - jnp.max(scores, axis=-1, keepdims=True)).astype(BF16)
        shifted_all[rows(s), :] = shifted
        state[s]["shifted"] = shifted

    def attend(s):
        cot_t = x[3 * hd :, rows(s)]
        cot = cot_t.T
        attended = matmul(state[s]["shifted"], v1[...], ((1,), (1,)))
        inverse = 1.0 / attended[:, hd : hd + 1]
        row_dot = jnp.sum(cot.astype(F32) * attended[:, 0:hd], axis=-1, keepdims=True) * inverse
        first, second, third = (t.astype(F32) for t in thirds(-row_dot))
        tail = jnp.where(
            lane == 0, first, jnp.where(lane == 1, second, jnp.where(lane == 2, third, 0.0))
        ).astype(BF16)
        difference = matmul(jnp.concatenate([cot, tail], axis=1), v1[...])
        state[s].update(cot_t=cot_t, inverse=inverse, difference=difference)

    def grad_score(s):
        grad_scores = (state[s]["shifted"].astype(F32) * state[s].pop("difference")).astype(BF16)
        scores_all[rows(s), :] = grad_scores
        state[s]["grad_scores"] = grad_scores

    def grad_query(s):
        inverse = state[s]["inverse"]
        product = matmul(state[s]["grad_scores"], k3[0:hd, :], ((1,), (1,))) * (inverse * scale)
        grads[0:hd, rows(s)] = product.T.astype(BF16)
        inverse_t = jnp.broadcast_to(inverse, (sub, LANES)).T[0:1, :]
        query_scaled[:, rows(s)] = (state[s]["query"] * (inverse_t * scale)).astype(BF16)
        cot_scaled[:, rows(s)] = (state[s]["cot_t"].astype(F32) * inverse_t).astype(BF16)
        state[s].clear()

    def both(stage, pair):
        for s in (2 * pair, 2 * pair + 1):
            if s < blocks:
                stage(s)

    both(score, 0)
    both(exponent, 0)
    for pair in range(blocks // 2):
        both(score, pair + 1)
        both(attend, pair)
        both(exponent, pair + 1)
        both(grad_score, pair)
        both(grad_query, pair)
    grads[hd : 2 * hd, :] = matmul(query_scaled[...], scores_all[...]).astype(BF16)
    grads[2 * hd : 3 * hd, :] = matmul(cot_scaled[...], shifted_all[...]).astype(BF16)
    grads[3 * hd :, :] = jnp.zeros((grads.shape[0] - 3 * hd, count), BF16)
    total = None
    for at in range(0, pieces, join):
        tokens = jnp.concatenate([chunk[...] for chunk in chunks[at : at + join]], axis=0)
        term = matmul(grads[:, at * width : (at + join) * width], tokens)
        total = term if total is None else total + term
    out_ref[...] = total.astype(BF16)


def head_gradient(order, cot, weight, chunks, rows):
    pieces, _, width = cot.shape
    count = pieces * width
    vmem = pl.BlockSpec(memory_space=pltpu.VMEM)
    return pl.pallas_call(
        functools.partial(head_kernel, 256),
        out_shape=jax.ShapeDtypeStruct((rows, chunks[0].shape[1]), BF16),
        in_specs=[pl.BlockSpec(memory_space=pltpu.SMEM)] + [vmem] * (2 + pieces),
        out_specs=vmem,
        scratch_shapes=[
            pltpu.VMEM((4 * HEAD_DIM, count), BF16),
            pltpu.VMEM((3 * HEAD_DIM, count), BF16),
            pltpu.VMEM((LANES, count), BF16),
            pltpu.VMEM((rows, count), BF16),
            pltpu.VMEM((HEAD_DIM, count), BF16),
            pltpu.VMEM((HEAD_DIM, count), BF16),
            pltpu.VMEM((count, count), BF16),
            pltpu.VMEM((count, count), BF16),
        ],
        compiler_params=pltpu.CompilerParams(vmem_limit_bytes=42 << 20),
        cost_estimate=pl.CostEstimate(
            flops=12 * count * count * LANES, bytes_accessed=8 << 20, transcendentals=count * count
        ),
        name="head_gradient",
    )(order, cot, weight, *chunks)


def exchange(array, axis_name):
    return lax.all_to_all(array, axis_name, split_axis=0, concat_axis=0, tiled=True)


RING, CORES = 4, 2


def gather_pieces(own, weight, cot):
    count = lax.axis_size("seq")
    me = lax.axis_index("seq")

    def over(index, dz, dx, dc):
        plane, x, core = index // (RING * CORES), index // CORES % RING, index % CORES
        return (plane ^ dz) * RING * CORES + (x + dx) % RING * CORES + (core ^ dc)

    def send(array, *by):
        return lax.ppermute(array, "seq", [(i, over(i, *by)) for i in range(count)])

    other = send(own, 1, 0, 0)
    right, left = send(own, 0, 1, 0), send(own, 0, -1, 0)
    other_left = send(other, 0, -1, 0)
    other_right = send(right, 1, 0, 0)
    right, weight = lax.optimization_barrier((right, weight))
    across = send(right, 0, 1, 0)
    other_right, other_left = lax.optimization_barrier((other_right, other_left))
    other_across = send(other_left, 0, -1, 0)
    across, cot = lax.optimization_barrier((across, exchange(cot, "seq")))
    near = [own, other, right, left, other_right, other_left, across, other_across]
    places = [(0, 0), (1, 0), (0, -1), (0, 1), (1, -1), (1, 1), (0, -2), (1, 2)]
    pieces, order = list(near), [over(me, dz, dx, 0) for dz, dx in places]
    for array, (dz, dx) in zip(near, places):
        pieces.append(send(array, 0, 0, 1))
        order.append(over(me, dz, dx, 1))
    return pieces, jnp.stack(order).astype(jnp.int32), weight, cot


def body(frames, map_weight, qkv_weight, cotangent):
    seq, dp = lax.axis_size("seq"), lax.axis_size("dp")
    columns = qkv_weight.shape[1] // seq
    padded = -(-columns // (16 * dp)) * 16 * dp
    normed, send = learn_tokens(frames[0], map_weight, cotangent[0], seq)
    own_weight = lax.dynamic_slice_in_dim(qkv_weight, lax.axis_index("seq") * columns, columns, 1)
    pieces, order, own_weight, cot = gather_pieces(normed, own_weight, send)
    term = head_gradient(order, cot, own_weight, pieces, padded)
    parts = exchange(term.reshape(dp, -1, term.shape[1]), "dp")
    summed = jnp.sum(parts.astype(F32), axis=0).astype(BF16)
    whole = exchange(jnp.broadcast_to(summed[None], (dp,) + summed.shape), "dp")
    return whole.reshape(term.shape)[:columns].astype(F32).T


def solution(mesh):
    placed = (P("dp", "seq", None, None), P(), P(), P("dp", "seq", None))
    return jax.shard_map(
        body, mesh=mesh, in_specs=placed, out_specs=P(None, "seq"), check_vma=False
    )
```

```python
import functools
import math

import jax
import jax.numpy as jnp
from jax import lax
from jax.experimental import pallas as pl
from jax.experimental.pallas import tpu as pltpu
from jax.sharding import PartitionSpec as P

HEAD_DIM = 80
F32, BF16 = jnp.float32, jnp.bfloat16
LANES = 128


def matmul(a, b, dims=((1,), (0,))):
    return lax.dot_general(a, b, (dims, ((), ())), preferred_element_type=F32)


def thirds(value):
    high = value.astype(BF16)
    rest = value - high.astype(F32)
    middle = rest.astype(BF16)
    return high, middle, (rest - middle.astype(F32)).astype(BF16)


def tokens_kernel(
    group, ahead, frames, map_weight, cot, normed, send, held, map_weight_t, cot_held, pooled, sems, own_sems
):
    count = frames.shape[0]
    slots = map_weight_t.shape[0]
    step = count // sems.shape[0]
    parts = [pl.ds(i * step, step) for i in range(sems.shape[0])]
    loads = [
        pltpu.make_async_copy(frames.at[part], held.at[part], sems.at[i])
        for i, part in enumerate(parts)
    ]
    map_load = pltpu.make_async_copy(map_weight, map_weight_t, own_sems.at[0])
    cot_load = pltpu.make_async_copy(cot, cot_held, own_sems.at[1])
    map_load.start()
    waiting = loads + [cot_load]
    for load in waiting[:ahead]:
        load.start()
    waiting = waiting[ahead:]
    map_load.wait()
    for g in range(count // group):
        for load in loads[g * group // step : (g + 1) * group // step]:
            load.wait()
            if waiting:
                waiting.pop(0).start()
        blocks = [held[g * group + k] for k in range(group)]
        logits = [matmul(map_weight_t[...], block, ((1,), (1,))) for block in blocks]
        maps = [jax.nn.sigmoid(l).astype(BF16) for l in logits]
        at = g * group * slots
        pooled[at : at + group * slots, :] = jnp.concatenate(
            [matmul(m, block) for m, block in zip(maps, blocks)], axis=0
        )
    for load in waiting:
        load.start()
    centred = pooled[...] - jnp.mean(pooled[...], axis=-1, keepdims=True)
    variance = jnp.mean(centred * centred, axis=-1, keepdims=True)
    normed[...] = (centred * lax.rsqrt(variance + 1e-06)).astype(BF16)
    cot_load.wait()
    send[...] = cot_held[...].T.reshape(send.shape)


def learn_tokens(frames, map_weight, cot, heads):
    count = frames.shape[0]
    tokens, width = cot.shape
    vmem, hbm = pl.BlockSpec(memory_space=pltpu.VMEM), pl.BlockSpec(memory_space=pltpu.HBM)
    return pl.pallas_call(
        functools.partial(tokens_kernel, math.gcd(count, 4), 4),
        out_shape=(
            jax.ShapeDtypeStruct((tokens, width), BF16),
            jax.ShapeDtypeStruct((heads, width // heads, tokens), BF16),
        ),
        in_specs=[hbm, hbm, hbm],
        out_specs=(vmem, vmem),
        scratch_shapes=[
            pltpu.VMEM(frames.shape, BF16),
            pltpu.VMEM(map_weight.shape[::-1], BF16),
            pltpu.VMEM(cot.shape, BF16),
            pltpu.VMEM(cot.shape, F32),
            pltpu.SemaphoreType.DMA((count // math.gcd(count, 2),)),
            pltpu.SemaphoreType.DMA((2,)),
        ],
        compiler_params=pltpu.CompilerParams(vmem_limit_bytes=62 << 20),
        name="learn_tokens",
    )(frames, map_weight.T, cot)


def head_kernel(sub, order_ref, cot_ref, weight_ref, *refs):
    pieces = cot_ref.shape[0]
    chunks, out_ref = refs[:pieces], refs[pieces]
    x, k3, v1, grads, query_scaled, cot_scaled, shifted_all, scores_all = refs[pieces + 1 :]
    hd = HEAD_DIM
    scale = 1.0 / math.sqrt(hd)
    width = cot_ref.shape[2]
    count = pieces * width
    join = 4
    for piece in range(pieces):
        x[3 * hd :, piece * width : (piece + 1) * width] = cot_ref[order_ref[piece]]
    weight_t = weight_ref[...].T
    for at in range(0, pieces, join):
        tokens = jnp.concatenate([chunk[...] for chunk in chunks[at : at + join]], axis=0)
        columns = slice(at * width, (at + join) * width)
        x[0 : 3 * hd, columns] = matmul(weight_t, tokens, ((1,), (1,))).astype(BF16)
    key = x[hd : 2 * hd, :]
    k3[...] = jnp.concatenate([key, key, key], axis=0)
    row = lax.broadcasted_iota(jnp.int32, (LANES - hd, count), 0)
    ones = jnp.where(row < 3, 1.0, 0.0).astype(BF16)
    v1[...] = jnp.concatenate([x[2 * hd : 3 * hd, :], ones], axis=0)
    lane = lax.broadcasted_iota(jnp.int32, (sub, LANES - hd), 1)
    blocks = count // sub
    state = [{} for _ in range(blocks)]

    def rows(s):
        return slice(s * sub, (s + 1) * sub)

    def score(s):
        query = x[0:hd, rows(s)].astype(F32)
        terms = jnp.concatenate(thirds(query * (scale * math.log2(math.e))), axis=0).T
        state[s].update(query=query, scores=matmul(terms, k3[...]))

    def exponent(s):
        scores = state[s].pop("scores")
        shifted = jnp.exp2(scores - jnp.max(scores, axis=-1, keepdims=True)).astype(BF16)
        shifted_all[rows(s), :] = shifted
        state[s]["shifted"] = shifted

    def attend(s):
        cot_t = x[3 * hd :, rows(s)]
        cot = cot_t.T
        attended = matmul(state[s]["shifted"], v1[...], ((1,), (1,)))
        inverse = 1.0 / attended[:, hd : hd + 1]
        row_dot = jnp.sum(cot.astype(F32) * attended[:, 0:hd], axis=-1, keepdims=True) * inverse
        first, second, third = (t.astype(F32) for t in thirds(-row_dot))
        tail = jnp.where(
            lane == 0, first, jnp.where(lane == 1, second, jnp.where(lane == 2, third, 0.0))
        ).astype(BF16)
        difference = matmul(jnp.concatenate([cot, tail], axis=1), v1[...])
        state[s].update(cot_t=cot_t, inverse=inverse, difference=difference)

    def grad_score(s):
        grad_scores = (state[s]["shifted"].astype(F32) * state[s].pop("difference")).astype(BF16)
        scores_all[rows(s), :] = grad_scores
        state[s]["grad_scores"] = grad_scores

    def grad_query(s):
        inverse = state[s]["inverse"]
        product = matmul(state[s]["grad_scores"], k3[0:hd, :], ((1,), (1,))) * (inverse * scale)
        grads[0:hd, rows(s)] = product.T.astype(BF16)
        inverse_t = jnp.broadcast_to(inverse, (sub, LANES)).T[0:1, :]
        query_scaled[:, rows(s)] = (state[s]["query"] * (inverse_t * scale)).astype(BF16)
        cot_scaled[:, rows(s)] = (state[s]["cot_t"].astype(F32) * inverse_t).astype(BF16)
        state[s].clear()

    def both(stage, pair):
        for s in (2 * pair, 2 * pair + 1):
            if s < blocks:
                stage(s)

    both(score, 0)
    both(exponent, 0)
    for pair in range(blocks // 2):
        both(score, pair + 1)
        both(attend, pair)
        both(exponent, pair + 1)
        both(grad_score, pair)
        both(grad_query, pair)
    grads[hd : 2 * hd, :] = matmul(query_scaled[...], scores_all[...]).astype(BF16)
    grads[2 * hd : 3 * hd, :] = matmul(cot_scaled[...], shifted_all[...]).astype(BF16)
    grads[3 * hd :, :] = jnp.zeros((grads.shape[0] - 3 * hd, count), BF16)
    total = None
    for at in range(0, pieces, join):
        tokens = jnp.concatenate([chunk[...] for chunk in chunks[at : at + join]], axis=0)
        term = matmul(grads[:, at * width : (at + join) * width], tokens)
        total = term if total is None else total + term
    out_ref[...] = total.astype(BF16)


def head_gradient(order, cot, weight, chunks, rows):
    pieces, _, width = cot.shape
    count = pieces * width
    vmem = pl.BlockSpec(memory_space=pltpu.VMEM)
    return pl.pallas_call(
        functools.partial(head_kernel, 256),
        out_shape=jax.ShapeDtypeStruct((rows, chunks[0].shape[1]), BF16),
        in_specs=[pl.BlockSpec(memory_space=pltpu.SMEM)] + [vmem] * (2 + pieces),
        out_specs=vmem,
        scratch_shapes=[
            pltpu.VMEM((4 * HEAD_DIM, count), BF16),
            pltpu.VMEM((3 * HEAD_DIM, count), BF16),
            pltpu.VMEM((LANES, count), BF16),
            pltpu.VMEM((rows, count), BF16),
            pltpu.VMEM((HEAD_DIM, count), BF16),
            pltpu.VMEM((HEAD_DIM, count), BF16),
            pltpu.VMEM((count, count), BF16),
            pltpu.VMEM((count, count), BF16),
        ],
        compiler_params=pltpu.CompilerParams(vmem_limit_bytes=42 << 20),
        cost_estimate=pl.CostEstimate(
            flops=12 * count * count * LANES, bytes_accessed=8 << 20, transcendentals=count * count
        ),
        name="head_gradient",
    )(order, cot, weight, *chunks)


def exchange(array, axis_name):
    return lax.all_to_all(array, axis_name, split_axis=0, concat_axis=0, tiled=True)


RING, CORES = 4, 2


def gather_pieces(own, weight, cot):
    count = lax.axis_size("seq")
    me = lax.axis_index("seq")

    def over(index, dz, dx, dc):
        plane, x, core = index // (RING * CORES), index // CORES % RING, index % CORES
        return (plane ^ dz) * RING * CORES + (x + dx) % RING * CORES + (core ^ dc)

    def send(array, *by):
        return lax.ppermute(array, "seq", [(i, over(i, *by)) for i in range(count)])

    other = send(own, 1, 0, 0)
    right, left = send(own, 0, 1, 0), send(own, 0, -1, 0)
    other, weight = lax.optimization_barrier((other, weight))
    other_left = send(other, 0, -1, 0)
    other_right = send(right, 1, 0, 0)
    across = send(right, 0, 1, 0)
    other_right, other_left = lax.optimization_barrier((other_right, other_left))
    other_across = send(other_left, 0, -1, 0)
    across, cot = lax.optimization_barrier((across, exchange(cot, "seq")))
    near = [own, other, right, left, other_right, other_left, across, other_across]
    places = [(0, 0), (1, 0), (0, -1), (0, 1), (1, -1), (1, 1), (0, -2), (1, 2)]
    pieces, order = list(near), [over(me, dz, dx, 0) for dz, dx in places]
    for array, (dz, dx) in zip(near, places):
        pieces.append(send(array, 0, 0, 1))
        order.append(over(me, dz, dx, 1))
    return pieces, jnp.stack(order).astype(jnp.int32), weight, cot


def body(frames, map_weight, qkv_weight, cotangent):
    seq, dp = lax.axis_size("seq"), lax.axis_size("dp")
    columns = qkv_weight.shape[1] // seq
    padded = -(-columns // (16 * dp)) * 16 * dp
    normed, send = learn_tokens(frames[0], map_weight, cotangent[0], seq)
    own_weight = lax.dynamic_slice_in_dim(qkv_weight, lax.axis_index("seq") * columns, columns, 1)
    pieces, order, own_weight, cot = gather_pieces(normed, own_weight, send)
    term = head_gradient(order, cot, own_weight, pieces, padded)
    parts = exchange(term.reshape(dp, -1, term.shape[1]), "dp")
    summed = jnp.sum(parts.astype(F32), axis=0).astype(BF16)
    whole = exchange(jnp.broadcast_to(summed[None], (dp,) + summed.shape), "dp")
    return whole.reshape(term.shape)[:columns].astype(F32).T


def solution(mesh):
    placed = (P("dp", "seq", None, None), P(), P(), P("dp", "seq", None))
    return jax.shard_map(
        body, mesh=mesh, in_specs=placed, out_specs=P(None, "seq"), check_vma=False
    )
```

```python
import functools
import math

import jax
import jax.numpy as jnp
from jax import lax
from jax.experimental import pallas as pl
from jax.experimental.pallas import tpu as pltpu
from jax.sharding import PartitionSpec as P

HEAD_DIM = 80
F32, BF16 = jnp.float32, jnp.bfloat16
LANES = 128


def matmul(a, b, dims=((1,), (0,))):
    return lax.dot_general(a, b, (dims, ((), ())), preferred_element_type=F32)


def thirds(value):
    high = value.astype(BF16)
    rest = value - high.astype(F32)
    middle = rest.astype(BF16)
    return high, middle, (rest - middle.astype(F32)).astype(BF16)


def tokens_kernel(
    group, ahead, frames, map_weight, cot, normed, send, held, map_weight_t, cot_held, pooled, sems, own_sems
):
    count = frames.shape[0]
    slots = map_weight_t.shape[0]
    step = count // sems.shape[0]
    parts = [pl.ds(i * step, step) for i in range(sems.shape[0])]
    loads = [
        pltpu.make_async_copy(frames.at[part], held.at[part], sems.at[i])
        for i, part in enumerate(parts)
    ]
    map_load = pltpu.make_async_copy(map_weight, map_weight_t, own_sems.at[0])
    cot_load = pltpu.make_async_copy(cot, cot_held, own_sems.at[1])
    map_load.start()
    waiting = loads + [cot_load]
    for load in waiting[:ahead]:
        load.start()
    waiting = waiting[ahead:]
    map_load.wait()
    for g in range(count // group):
        for load in loads[g * group // step : (g + 1) * group // step]:
            load.wait()
            if waiting:
                waiting.pop(0).start()
        blocks = [held[g * group + k] for k in range(group)]
        logits = [matmul(map_weight_t[...], block, ((1,), (1,))) for block in blocks]
        maps = [jax.nn.sigmoid(l).astype(BF16) for l in logits]
        at = g * group * slots
        pooled[at : at + group * slots, :] = jnp.concatenate(
            [matmul(m, block) for m, block in zip(maps, blocks)], axis=0
        )
    for load in waiting:
        load.start()
    centred = pooled[...] - jnp.mean(pooled[...], axis=-1, keepdims=True)
    variance = jnp.mean(centred * centred, axis=-1, keepdims=True)
    normed[...] = (centred * lax.rsqrt(variance + 1e-06)).astype(BF16)
    cot_load.wait()
    send[...] = cot_held[...].T.reshape(send.shape)


def learn_tokens(frames, map_weight, cot, heads):
    count = frames.shape[0]
    tokens, width = cot.shape
    vmem, hbm = pl.BlockSpec(memory_space=pltpu.VMEM), pl.BlockSpec(memory_space=pltpu.HBM)
    return pl.pallas_call(
        functools.partial(tokens_kernel, math.gcd(count, 4), 4),
        out_shape=(
            jax.ShapeDtypeStruct((tokens, width), BF16),
            jax.ShapeDtypeStruct((heads, width // heads, tokens), BF16),
        ),
        in_specs=[hbm, hbm, hbm],
        out_specs=(vmem, vmem),
        scratch_shapes=[
            pltpu.VMEM(frames.shape, BF16),
            pltpu.VMEM(map_weight.shape[::-1], BF16),
            pltpu.VMEM(cot.shape, BF16),
            pltpu.VMEM(cot.shape, F32),
            pltpu.SemaphoreType.DMA((count // math.gcd(count, 2),)),
            pltpu.SemaphoreType.DMA((2,)),
        ],
        compiler_params=pltpu.CompilerParams(vmem_limit_bytes=62 << 20),
        name="learn_tokens",
    )(frames, map_weight.T, cot)


def head_kernel(sub, order_ref, cot_ref, weight_ref, *refs):
    pieces = cot_ref.shape[0]
    chunks, out_ref = refs[:pieces], refs[pieces]
    x, k3, v1, grads, query_scaled, cot_scaled, shifted_all, scores_all = refs[pieces + 1 :]
    hd = HEAD_DIM
    scale = 1.0 / math.sqrt(hd)
    width = cot_ref.shape[2]
    count = pieces * width
    join = 4
    for piece in range(pieces):
        x[3 * hd :, piece * width : (piece + 1) * width] = cot_ref[order_ref[piece]]
    weight_t = weight_ref[...].T
    for at in range(0, pieces, join):
        tokens = jnp.concatenate([chunk[...] for chunk in chunks[at : at + join]], axis=0)
        columns = slice(at * width, (at + join) * width)
        x[0 : 3 * hd, columns] = matmul(weight_t, tokens, ((1,), (1,))).astype(BF16)
    key = x[hd : 2 * hd, :]
    k3[...] = jnp.concatenate([key, key, key], axis=0)
    row = lax.broadcasted_iota(jnp.int32, (LANES - hd, count), 0)
    ones = jnp.where(row < 3, 1.0, 0.0).astype(BF16)
    v1[...] = jnp.concatenate([x[2 * hd : 3 * hd, :], ones], axis=0)
    lane = lax.broadcasted_iota(jnp.int32, (sub, LANES - hd), 1)
    blocks = count // sub
    state = [{} for _ in range(blocks)]

    def rows(s):
        return slice(s * sub, (s + 1) * sub)

    def score(s):
        query = x[0:hd, rows(s)].astype(F32)
        terms = jnp.concatenate(thirds(query * (scale * math.log2(math.e))), axis=0).T
        state[s].update(query=query, scores=matmul(terms, k3[...]))

    def exponent(s):
        scores = state[s].pop("scores")
        shifted = jnp.exp2(scores - jnp.max(scores, axis=-1, keepdims=True)).astype(BF16)
        shifted_all[rows(s), :] = shifted
        state[s]["shifted"] = shifted

    def attend(s):
        cot_t = x[3 * hd :, rows(s)]
        cot = cot_t.T
        attended = matmul(state[s]["shifted"], v1[...], ((1,), (1,)))
        inverse = 1.0 / attended[:, hd : hd + 1]
        row_dot = jnp.sum(cot.astype(F32) * attended[:, 0:hd], axis=-1, keepdims=True) * inverse
        first, second, third = (t.astype(F32) for t in thirds(-row_dot))
        tail = jnp.where(
            lane == 0, first, jnp.where(lane == 1, second, jnp.where(lane == 2, third, 0.0))
        ).astype(BF16)
        difference = matmul(jnp.concatenate([cot, tail], axis=1), v1[...])
        inverse_t = jnp.broadcast_to(inverse, (sub, LANES)).T[0:1, :]
        cot_scaled[:, rows(s)] = (cot_t.astype(F32) * inverse_t).astype(BF16)
        state[s].update(inverse=inverse, inverse_t=inverse_t, difference=difference)

    def grad_score(s):
        grad_scores = (state[s]["shifted"].astype(F32) * state[s].pop("difference")).astype(BF16)
        scores_all[rows(s), :] = grad_scores
        state[s]["grad_scores"] = grad_scores

    def grad_query(s):
        inverse = state[s]["inverse"]
        product = matmul(state[s]["grad_scores"], k3[0:hd, :], ((1,), (1,))) * (inverse * scale)
        grads[0:hd, rows(s)] = product.T.astype(BF16)
        inverse_t = state[s]["inverse_t"]
        query_scaled[:, rows(s)] = (state[s]["query"] * (inverse_t * scale)).astype(BF16)
        state[s].clear()

    def both(stage, pair):
        for s in (2 * pair, 2 * pair + 1):
            if s < blocks:
                stage(s)

    both(score, 0)
    both(exponent, 0)
    for pair in range(blocks // 2):
        both(score, pair + 1)
        both(attend, pair)
        both(exponent, pair + 1)
        if pair == blocks // 2 - 1:
            grads[2 * hd : 3 * hd, :] = matmul(cot_scaled[...], shifted_all[...]).astype(BF16)
        both(grad_score, pair)
        both(grad_query, pair)
    grads[hd : 2 * hd, :] = matmul(query_scaled[...], scores_all[...]).astype(BF16)
    grads[3 * hd :, :] = jnp.zeros((grads.shape[0] - 3 * hd, count), BF16)
    total = None
    for at in range(0, pieces, join):
        tokens = jnp.concatenate([chunk[...] for chunk in chunks[at : at + join]], axis=0)
        term = matmul(grads[:, at * width : (at + join) * width], tokens)
        total = term if total is None else total + term
    out_ref[...] = total.astype(BF16)


def head_gradient(order, cot, weight, chunks, rows):
    pieces, _, width = cot.shape
    count = pieces * width
    vmem = pl.BlockSpec(memory_space=pltpu.VMEM)
    return pl.pallas_call(
        functools.partial(head_kernel, 256),
        out_shape=jax.ShapeDtypeStruct((rows, chunks[0].shape[1]), BF16),
        in_specs=[pl.BlockSpec(memory_space=pltpu.SMEM)] + [vmem] * (2 + pieces),
        out_specs=vmem,
        scratch_shapes=[
            pltpu.VMEM((4 * HEAD_DIM, count), BF16),
            pltpu.VMEM((3 * HEAD_DIM, count), BF16),
            pltpu.VMEM((LANES, count), BF16),
            pltpu.VMEM((rows, count), BF16),
            pltpu.VMEM((HEAD_DIM, count), BF16),
            pltpu.VMEM((HEAD_DIM, count), BF16),
            pltpu.VMEM((count, count), BF16),
            pltpu.VMEM((count, count), BF16),
        ],
        compiler_params=pltpu.CompilerParams(vmem_limit_bytes=42 << 20),
        cost_estimate=pl.CostEstimate(
            flops=12 * count * count * LANES, bytes_accessed=8 << 20, transcendentals=count * count
        ),
        name="head_gradient",
    )(order, cot, weight, *chunks)


def exchange(array, axis_name):
    return lax.all_to_all(array, axis_name, split_axis=0, concat_axis=0, tiled=True)


RING, CORES = 4, 2


def gather_pieces(own, weight, cot):
    count = lax.axis_size("seq")
    me = lax.axis_index("seq")

    def over(index, dz, dx, dc):
        plane, x, core = index // (RING * CORES), index // CORES % RING, index % CORES
        return (plane ^ dz) * RING * CORES + (x + dx) % RING * CORES + (core ^ dc)

    def send(array, *by):
        return lax.ppermute(array, "seq", [(i, over(i, *by)) for i in range(count)])

    other = send(own, 1, 0, 0)
    right, left = send(own, 0, 1, 0), send(own, 0, -1, 0)
    other, weight = lax.optimization_barrier((other, weight))
    other_left = send(other, 0, -1, 0)
    other_right = send(right, 1, 0, 0)
    across = send(right, 0, 1, 0)
    other_right, other_left = lax.optimization_barrier((other_right, other_left))
    other_across = send(other_left, 0, -1, 0)
    across, cot = lax.optimization_barrier((across, exchange(cot, "seq")))
    near = [own, other, right, left, other_right, other_left, across, other_across]
    places = [(0, 0), (1, 0), (0, -1), (0, 1), (1, -1), (1, 1), (0, -2), (1, 2)]
    pieces, order = list(near), [over(me, dz, dx, 0) for dz, dx in places]
    for array, (dz, dx) in zip(near, places):
        pieces.append(send(array, 0, 0, 1))
        order.append(over(me, dz, dx, 1))
    return pieces, jnp.stack(order).astype(jnp.int32), weight, cot


def body(frames, map_weight, qkv_weight, cotangent):
    seq, dp = lax.axis_size("seq"), lax.axis_size("dp")
    columns = qkv_weight.shape[1] // seq
    padded = -(-columns // (16 * dp)) * 16 * dp
    normed, send = learn_tokens(frames[0], map_weight, cotangent[0], seq)
    own_weight = lax.dynamic_slice_in_dim(qkv_weight, lax.axis_index("seq") * columns, columns, 1)
    pieces, order, own_weight, cot = gather_pieces(normed, own_weight, send)
    term = head_gradient(order, cot, own_weight, pieces, padded)
    parts = exchange(term.reshape(dp, -1, term.shape[1]), "dp")
    summed = jnp.sum(parts.astype(F32), axis=0).astype(BF16)
    whole = exchange(jnp.broadcast_to(summed[None], (dp,) + summed.shape), "dp")
    return whole.reshape(term.shape)[:columns].astype(F32).T


def solution(mesh):
    placed = (P("dp", "seq", None, None), P(), P(), P("dp", "seq", None))
    return jax.shard_map(
        body, mesh=mesh, in_specs=placed, out_specs=P(None, "seq"), check_vma=False
    )
```
